128 devices in a mesh: seq: 32 (over y, x, core), tp: 4 (over z).
Axes of the slice: x: 4, y: 4, z: 4, core: 2. Of those that a mesh axis runs over, the one named last changes fastest.
Arguments:
- seg_tokens: bfloat16 [32768, 3, 4096], P('seq', None, 'tp'), may hold values from -6 to 6
- seg_length: int32 [32], P('seq'), may hold values from 0 to 1024, as said below
- seg_offset: int32 [32], P('seq'), may hold values from 0 to 16128, as said below
- short_weight: float32 [3, 3, 4096], P(None, None, 'tp'), may hold values from -3.5 to 3.5
- residues: float32 [16, 4096], P(None, 'tp'), may hold values from -4 to 4
- filter_span: float32 [16, 4096], P(None, 'tp'), may hold values from 30 to 65536
- skip_gain: float32 [4096], P('tp'), may hold values from -4 to 4
- out_weight: bfloat16 [4096, 4096], P('tp'), may hold values from -0.09375 to 0.09375
Outputs:
- mixed: bfloat16 [16384, 4096], P(('seq', 'tp'))
The draws below stay inside these ranges and needn't reach their ends.
Inputs may be any that keep to these rules, and one draw needn't show every extreme that they name: Segment s has seg_length[s] valid rows at the head of its buffer; the segments laid end to end in order cover the 16384 positions exactly, and each segment's first and last position lie within 256 positions of s * 512 and (s + 1) * 512 - 1. seg_offset[s] is the sum of seg_length over the segments before s.
All inputs are finite; a program needn't handle non-finite values.
Results may differ from the reference program's by a relative error of at most 0.02.
Values may be sent and summed in bfloat16 or wider, within the bound.
A program may use at most 128 MiB of HBM per device.

```python
import jax
import jax.numpy as jnp
from jax import lax

D = 4096
TOK_DEV = 512
ORDER = 16
SHORT = 3
SEGMENTS = 32
BUF_ROWS = 32768
TOKENS = 16384
FFT_LEN = 32768


def segment_bounds(key):
    half_rows = TOK_DEV // 2
    first_key, second_key = jax.random.split(key)
    drift = jax.random.randint(first_key, (SEGMENTS + 1,), -half_rows, half_rows + 1, dtype=jnp.int32)
    chosen = jax.random.randint(second_key, (), 1, SEGMENTS - 1, dtype=jnp.int32)
    places = jnp.arange(SEGMENTS + 1, dtype=jnp.int32)
    drift = jnp.where(places == SEGMENTS - 1, half_rows, drift)
    drift = jnp.where(places == chosen, -half_rows, drift)
    drift = jnp.where(places == chosen + 1, half_rows, drift)
    drift = jnp.where((places == 0) | (places == SEGMENTS), 0, drift)
    return (places * TOK_DEV + drift).astype(jnp.int32)


def draw_seg_length(key, part):
    bounds = segment_bounds(key)
    return (bounds[1:] - bounds[:-1]).astype(jnp.int32)


def draw_seg_offset(key, part):
    bounds = segment_bounds(key)
    return bounds[:-1].astype(jnp.int32)


def log_spread(key, lower, upper):
    unit = jax.random.uniform(key, (ORDER, D), jnp.float32)
    return jnp.exp(jnp.log(lower) + unit * (jnp.log(upper) - jnp.log(lower)))


def draw_filter_span(key, part):
    key = jax.random.fold_in(key, 7)
    return log_spread(key, 30.0, float(4 * TOKENS)).astype(jnp.float32)


def block_scale(own_key, extent, pieces, low, top_value):
    level, own = 1.0, jax.random.fold_in(own_key, 6)
    for axis_at, shards_of in pieces:
        steps = jnp.exp(jax.random.uniform(jax.random.fold_in(own, axis_at), (shards_of,), jnp.float32, low / len(pieces), top_value / len(pieces)))
        level = level * jnp.repeat(steps, extent[axis_at] // shards_of).reshape([-1 if axis == axis_at else 1 for axis in range(len(extent))])
    return level


def bell_draw(own_key, shape, spread, reach, cuts=(), held_as=jnp.bfloat16):
    array = jax.random.normal(own_key, shape, jnp.float32) * spread
    if len(cuts) > 0:
        array = block_scale(own_key, shape, cuts, -0.22, 0.18) * array
    return jnp.clip(array, min=-reach, max=reach).astype(held_as)


def setup_inputs(seed: int = 0) -> dict:
    key_list = jax.random.split(jax.random.key(seed), 9)
    seg_tokens = bell_draw(key_list[0], (BUF_ROWS, 3, D), 1.0, 6.0, ((0, 32), (2, 4)))
    seg_length = draw_seg_length(jax.random.fold_in(key_list[8], 71), 0)
    seg_offset = draw_seg_offset(jax.random.fold_in(key_list[8], 71), 0)
    short_weight = bell_draw(key_list[3], (SHORT, 3, D), 3 ** -0.5, 3.5, ((2, 4),), jnp.float32)
    residues = bell_draw(key_list[4], (ORDER, D), 0.25, 4.0, ((1, 4),), jnp.float32)
    filter_span = draw_filter_span(jax.random.fold_in(key_list[8], 71), 0)
    skip_gain = bell_draw(key_list[6], (D,), 1.0, 4.0, ((0, 4),), jnp.float32)
    out_weight = bell_draw(key_list[7], (D, D), D ** -0.5, 0.09375, ((0, 4),))
    return {"seg_tokens": seg_tokens, "seg_length": seg_length, "seg_offset": seg_offset, "short_weight": short_weight, "residues": residues, "filter_span": filter_span, "skip_gain": skip_gain, "out_weight": out_weight}


def reference(seg_tokens, seg_length, seg_offset, short_weight, residues, filter_span, skip_gain, out_weight):
    buffer_rows = seg_tokens.shape[0] // SEGMENTS
    ends = seg_offset + seg_length
    positions = jnp.arange(TOKENS, dtype=jnp.int32)
    source = lax.optimization_barrier(jnp.sum((ends[None, :] <= positions[:, None]).astype(jnp.int32), axis=1)).astype(jnp.int32)
    source_row = (source * buffer_rows + positions - seg_offset[source]).astype(jnp.int32)
    block = min(256, D)
    block_count = D // block
    times_f = jnp.arange(TOKENS, dtype=jnp.int32).astype(jnp.float32)

    def one_block(block_id):
        first = (block_id * block).astype(jnp.int32)
        columns = lax.dynamic_slice_in_dim(seg_tokens, first, block, 2)
        picked = jnp.take(columns, source_row, axis=0).astype(jnp.float32)
        taps = lax.dynamic_slice_in_dim(short_weight, first, block, 2)
        padded = jnp.pad(picked, ((SHORT - 1, 0), (0, 0), (0, 0)))
        features = jnp.zeros((TOKENS, 3, block), jnp.float32)
        for shift_id in range(SHORT):
            features = features + taps[shift_id] * padded[SHORT - 1 - shift_id:SHORT - 1 - shift_id + TOKENS]
        gated = (features[:, 1, :] * features[:, 2, :]).astype(jnp.bfloat16)
        weights_block = lax.dynamic_slice_in_dim(residues, first, block, 1)
        spans_block = lax.dynamic_slice_in_dim(filter_span, first, block, 1)
        filt = jnp.zeros((TOKENS, block), jnp.float32)
        for order_id in range(ORDER):
            rate = 1.0 / spans_block[order_id]
            filt = filt + weights_block[order_id] * jnp.sqrt(rate) * jnp.exp(-rate[None, :] * times_f[:, None])
        gated_f = gated.astype(jnp.float32)
        spectrum = jnp.fft.rfft(gated_f, n=FFT_LEN, axis=0) * jnp.fft.rfft(filt, n=FFT_LEN, axis=0)
        conv = jnp.fft.irfft(spectrum, n=FFT_LEN, axis=0)[:TOKENS]
        skip_block = lax.dynamic_slice_in_dim(skip_gain, first, block, 0)
        return (features[:, 0, :] * (conv + skip_block * gated_f)).astype(jnp.bfloat16)
    blocks = lax.map(one_block, jnp.arange(block_count, dtype=jnp.int32))
    mixer = jnp.transpose(blocks, (1, 0, 2)).reshape(TOKENS, D)
    return jnp.dot(mixer, out_weight, preferred_element_type=jnp.float32).astype(jnp.bfloat16)
```

```python
import functools

import jax
import jax.numpy as jnp
from jax import lax
from jax.experimental import pallas as pl
from jax.experimental.pallas import tpu as pltpu
from jax.sharding import PartitionSpec as P

F32 = jnp.float32
BF16 = jnp.bfloat16
LANES = 128
ROW_GROUP = 8
HEAD = 16
SUB = 4


def remote(src, dst, send_sem, recv_sem, **where):
    return pltpu.make_async_remote_copy(
        src_ref=src,
        dst_ref=dst,
        send_sem=send_sem,
        recv_sem=recv_sem,
        device_id=where,
        device_id_type=pl.DeviceIdType.MESH,
    )


def add_all(terms):
    while len(terms) > 1:
        terms = [a + b for a, b in zip(terms[::2], terms[1::2])] + (
            [terms[-1]] if len(terms) % 2 else []
        )
    return terms[0]


def kernel(
    n_seq,
    n_tp,
    len_ref,
    off_ref,
    x_hbm,
    taps_ref,
    res_ref,
    span_ref,
    skip_ref,
    w_hbm,
    out_ref,
    xq,
    xk,
    xv,
    w_ref,
    tail_out,
    tail_in,
    g_raw,
    f_raw,
    g_win,
    f_win,
    g_left,
    g_right,
    f_left,
    f_right,
    own_state,
    near_out,
    near_in,
    far_out,
    far_in,
    col_out,
    col_in,
    carry_ref,
    decay_t,
    weight_t,
    g_t,
    y_t,
    mix,
    cw_out,
    cw_in,
    ccw_out,
    ccw_in,
    load_sem,
    tail_ss,
    tail_rs,
    halo_ss,
    halo_rs,
    near_ss,
    near_rs,
    far_ss,
    far_rs,
    col_ss,
    col_rs,
    cw_ss,
    cw_rs,
    ccw_ss,
    ccw_rs,
):
    buf_rows = x_hbm.shape[1]
    rows = buf_rows // 2
    half = rows // 2
    chans = x_hbm.shape[2]
    modes = res_ref.shape[0]
    tiles = chans // LANES
    group = min(ROW_GROUP, n_seq)
    cols = n_seq // group
    s = lax.axis_index("seq")
    me = lax.axis_index("tp")
    row_id = lax.div(s, group)
    pos = lax.rem(s, group)

    def seq_at(k):
        return lax.rem(s + k + n_seq, n_seq)

    def mate(k):
        return row_id * group + lax.rem(pos + k, group)

    def below(k):
        return lax.rem(row_id + k, cols) * group + pos

    def tp_at(k):
        return lax.rem(me + k + n_tp, n_tp)

    loads = [
        pltpu.make_async_copy(x_hbm.at[j], ref.at[pl.ds(HEAD, buf_rows)], load_sem.at[j])
        for j, ref in ((1, xk), (2, xv), (0, xq))
    ]
    loads.append(pltpu.make_async_copy(w_hbm, w_ref, load_sem.at[3]))
    for copy in loads:
        copy.start()

    barrier = pltpu.get_barrier_semaphore()
    greeted = 0
    for k in (1, -1, 2, -2):
        pl.semaphore_signal(barrier, inc=1, device_id={"seq": seq_at(k)}, device_id_type=pl.DeviceIdType.MESH)
        greeted += 1
    for k in range(1, group):
        pl.semaphore_signal(barrier, inc=1, device_id={"seq": mate(k)}, device_id_type=pl.DeviceIdType.MESH)
        greeted += 1
    for k in range(1, cols):
        pl.semaphore_signal(barrier, inc=1, device_id={"seq": below(k)}, device_id_type=pl.DeviceIdType.MESH)
        greeted += 1
    for k in (1, -1):
        pl.semaphore_signal(barrier, inc=1, device_id={"tp": tp_at(k)}, device_id_type=pl.DeviceIdType.MESH)
        greeted += 1

    seg_len = len_ref[0]
    shift = off_ref[0] - (rows * s - half)

    for copy in loads[:3]:
        copy.wait()

    last_two = seg_len - 2 + lax.broadcasted_iota(jnp.int32, (HEAD, buf_rows), 0)
    have = lax.broadcasted_iota(jnp.int32, (HEAD, buf_rows), 1)
    pick_last = jnp.where(last_two == have, 1.0, 0.0).astype(BF16)
    for j, ref in enumerate((xq, xk, xv)):
        tail_out[pl.ds(2 * j, 2), :] = jnp.dot(
            pick_last, ref[pl.ds(HEAD, buf_rows), :], preferred_element_type=F32
        )[:2]
    tail_out[pl.ds(6, 2), :] = jnp.full((2, chans), jnp.minimum(seg_len, 2).astype(F32))

    pl.semaphore_wait(barrier, greeted)

    tails = [
        remote(tail_out, tail_in.at[k - 1], tail_ss.at[k - 1], tail_rs.at[k - 1], seq=seq_at(k))
        for k in (1, 2)
    ]
    for copy in tails:
        copy.start()
    def feature(ref, j, m, lane, width):
        block = ref[pl.ds(pl.multiple_of(16 * m, 16), 32), pl.ds(lane, width)].astype(F32)
        out = taps_ref[0, pl.ds(j, 1), pl.ds(lane, width)] * block[16:]
        for i in (1, 2):
            out += taps_ref[i, pl.ds(j, 1), pl.ds(lane, width)] * pltpu.roll(block, i, 0)[16:]
        return out

    width = 256

    def gate_rows(m, _):
        for lane in range(0, chans, width):
            gated = feature(xk, 1, m, lane, width) * feature(xv, 2, m, lane, width)
            g_raw[pl.ds(pl.multiple_of(16 * m, 16), 16), pl.ds(lane, width)] = gated.astype(BF16)
        return 0

    lax.fori_loop(1, buf_rows // 16, gate_rows, 0)

    for copy in tails:
        copy.wait_recv()
    count = tail_in[0, pl.ds(6, 1), :]
    row16 = lax.broadcasted_iota(jnp.int32, (HEAD, 1), 0)
    for j, ref in enumerate((xq, xk, xv)):
        prev_1, last_1 = tail_in[0, pl.ds(2 * j, 1), :], tail_in[0, pl.ds(2 * j + 1, 1), :]
        prev_2, last_2 = tail_in[1, pl.ds(2 * j, 1), :], tail_in[1, pl.ds(2 * j + 1, 1), :]
        prev_2, last_2 = jnp.where(s > 1, prev_2, 0.0), jnp.where(s > 1, last_2, 0.0)
        last = jnp.where(count > 0.5, last_1, last_2)
        prev = jnp.where(count > 1.5, prev_1, jnp.where(count > 0.5, last_2, prev_2))
        last, prev = jnp.where(s > 0, last, 0.0), jnp.where(s > 0, prev, 0.0)
        ref[pl.ds(0, HEAD), :] = jnp.where(
            row16 == HEAD - 1, last, jnp.where(row16 == HEAD - 2, prev, 0.0)
        ).astype(BF16)

    gate_rows(0, 0)

    def align(src, dst, b):
        first = max(0, b * LANES - rows)
        span = (b + 1) * LANES - first
        want = b * LANES - shift + lax.broadcasted_iota(jnp.int32, (LANES, span), 0)
        have = first + lax.broadcasted_iota(jnp.int32, (LANES, span), 1)
        pick = jnp.where((want == have) & (have < seg_len), 1.0, 0.0).astype(BF16)
        dst[pl.ds(b * LANES, LANES), :] = jnp.dot(
            pick, src[pl.ds(first, span), :], preferred_element_type=F32
        ).astype(BF16)

    def align_range(src, dst, first, stop):
        for b in range(first, stop):
            align(src, dst, b)

    side = half // LANES
    whole = buf_rows // LANES

    def window(src, dst, left, right, k):
        align_range(src, dst, 0, side)
        to_left = remote(
            dst.at[pl.ds(0, half)], right, halo_ss.at[k], halo_rs.at[k], seq=seq_at(-1)
        )
        to_left.start()
        align_range(src, dst, whole - side, whole)
        to_right = remote(
            dst.at[pl.ds(buf_rows - half, half)],
            left,
            halo_ss.at[k + 1],
            halo_rs.at[k + 1],
            seq=seq_at(1),
        )
        to_right.start()
        align_range(src, dst, side, whole - side)
        return [to_left, to_right]

    halos_g = window(g_raw, g_win, g_left, g_right, 0)

    sub8 = lax.broadcasted_iota(jnp.int32, (8, 1), 0).astype(F32)

    def states(j, _):
        lane = pl.ds(pl.multiple_of(j * LANES, LANES), LANES)
        rate = 1.0 / span_ref[:, lane]
        decay8 = jnp.exp(-8.0 * rate)
        step8 = [jnp.broadcast_to(decay8[r : r + 1], (8, LANES)) for r in range(modes)]

        def rows16(m, held):
            g = g_win[pl.ds(pl.multiple_of(16 * m, 16), 16), lane].astype(F32)
            held = [h * d + g[:8] for h, d in zip(held, step8)]
            return [h * d + g[8:] for h, d in zip(held, step8)]

        def put(ref, held):
            for r in range(modes):
                fold = jnp.exp((sub8 - 8.0) * rate[r : r + 1])
                ref[pl.ds(r, 1), lane] = jnp.sum(held[r] * fold, axis=0, keepdims=True)

        held = [jnp.zeros((8, LANES), F32)] * modes
        held = lax.fori_loop(0, half // 16, rows16, held)
        put(own_state, held)
        held = lax.fori_loop(half // 16, (half + rows) // 16, rows16, held)
        put(near_out, held)
        held = lax.fori_loop((half + rows) // 16, buf_rows // 16, rows16, held)
        put(far_out, held)
        return 0

    lax.fori_loop(0, tiles, states, 0)

    rate = 1.0 / span_ref[...]
    far_out[...] = far_out[...] * jnp.exp(float(half - rows) * rate)

    near = remote(near_out, near_in, near_ss, near_rs, seq=seq_at(1))
    near.start()
    fars = [
        remote(far_out, far_in.at[k - 1], far_ss.at[k - 1], far_rs.at[k - 1], seq=mate(k))
        for k in range(1, group)
    ]
    for copy in fars:
        copy.start()

    def query_rows(m, _):
        for lane in range(0, chans, width):
            f_raw[pl.ds(pl.multiple_of(16 * m, 16), 16), pl.ds(lane, width)] = feature(
                xq, 0, m, lane, width
            ).astype(BF16)
        return 0

    lax.fori_loop(0, buf_rows // 16, query_rows, 0)
    halos_f = window(f_raw, f_win, f_left, f_right, 2)

    def powers(blocks):
        return jnp.exp((-float(rows) * blocks.astype(F32)) * rate)

    for copy in fars:
        copy.wait_recv()
    carry = jnp.zeros_like(rate)
    row_sum = powers(group - 1 - pos) * far_out[...]
    row_short = jnp.where(
        pos < group - 1, powers(jnp.maximum(group - 2 - pos, 0)) * far_out[...], 0.0
    )
    for k in range(1, group):
        source = lax.rem(pos - k + group, group)
        piece = far_in[k - 1]
        row_sum += powers(group - 1 - source) * piece
        row_short += jnp.where(
            source < group - 1, powers(jnp.maximum(group - 2 - source, 0)) * piece, 0.0
        )
        if k >= 2:
            carry += jnp.where(k <= pos, powers(jnp.int32(k - 2)) * piece, 0.0)
    col_out[0] = jnp.where(pos == 0, row_short, powers(jnp.maximum(pos - 1, 0)) * row_sum)
    col_out[1] = powers(group + pos - 1) * row_sum
    downs = [
        remote(
            col_out.at[min(k - 1, 1)],
            col_in.at[k - 1],
            col_ss.at[k - 1],
            col_rs.at[k - 1],
            seq=below(k),
        )
        for k in range(1, cols)
    ]
    for copy in downs:
        copy.start()

    for copy in halos_g:
        copy.wait_recv()
    g_own = g_win.at[pl.ds(half, rows)]
    f_own = f_win.at[pl.ds(half, rows)]

    def join(own, left, right):
        def step(m, _):
            at = pl.ds(pl.multiple_of(16 * m, 16), 16)
            low = pl.ds(pl.multiple_of(half + 16 * m, 16), 16)
            high = pl.ds(pl.multiple_of(rows + 16 * m, 16), 16)
            own[low, :] = own[low, :] + left[at, :]
            own[high, :] = own[high, :] + right[at, :]
            return 0

        lax.fori_loop(0, half // 16, step, 0)

    join(g_win, g_left, g_right)
    decay1 = jnp.exp(-rate)
    weight = res_ref[...] * jnp.sqrt(rate)
    for j in range(tiles):
        decay_t[pl.ds(j, modes, stride=tiles), :] = decay1[:, j * LANES : (j + 1) * LANES]
        weight_t[pl.ds(j, modes, stride=tiles), :] = weight[:, j * LANES : (j + 1) * LANES]

    def spread(m, _):
        block = g_own[pl.ds(pl.multiple_of(16 * m, 16), 16), :].astype(F32)
        for j in range(tiles):
            g_t[pl.ds(16 * tiles * m + j, 16, stride=tiles), :] = block[
                :, j * LANES : (j + 1) * LANES
            ]
        return 0

    lax.fori_loop(0, rows // 16, spread, 0)

    decays = [decay_t[pl.ds(r * tiles, tiles), :] for r in range(modes)]
    weights = [weight_t[pl.ds(r * tiles, tiles), :] for r in range(modes)]

    def token(t, held):
        at = pl.ds(pl.multiple_of(t * tiles, tiles), tiles)
        g = g_t[at, :]
        held = [h * d + g for h, d in zip(held, decays)]
        y_t[at, :] = add_all([h * w for h, w in zip(held, weights)])
        return held

    lax.fori_loop(0, rows, token, [jnp.zeros((tiles, LANES), F32)] * modes, unroll=4)

    near.wait_recv()
    carry += own_state[...]
    carry += jnp.where(s > 0, near_in[...], 0.0)
    for k, copy in enumerate(downs, 1):
        copy.wait_recv()
        piece = col_in[k - 1]
        if k > 2:
            piece = piece * jnp.exp(-float(rows * group * (k - 2)) * rate)
        carry += jnp.where(k <= row_id, piece, 0.0)
    carry_ref[...] = carry * weight

    for copy in halos_f:
        copy.wait_recv()
    join(f_win, f_left, f_right)
    loads[3].wait()

    block_rows = rows // n_tp

    def mix_block(d):
        first = d * block_rows

        def tile(j, _):
            lane = pl.ds(pl.multiple_of(j * LANES, LANES), LANES)
            rate_j = 1.0 / span_ref[:, lane]
            decay8 = jnp.exp(-8.0 * rate_j)
            state = carry_ref[:, lane]
            skip = skip_ref[:, lane]
            ahead = sub8 + first.astype(F32)
            parts = [
                state[r : r + 1] * jnp.exp(-ahead * rate_j[r : r + 1]) for r in range(modes)
            ]
            step8 = [jnp.broadcast_to(decay8[r : r + 1], (8, LANES)) for r in range(modes)]

            def rows16(m, parts):
                row = pl.multiple_of(first + 16 * m, 16)
                g = g_own[pl.ds(row, 16), lane].astype(F32)
                f = f_own[pl.ds(row, 16), lane].astype(F32)
                done = []
                for k in range(2):
                    local = y_t[pl.ds((row + 8 * k) * tiles + j, 8, stride=tiles), :]
                    conv = local + add_all(parts)
                    done.append(f[8 * k : 8 * k + 8] * (conv + skip * g[8 * k : 8 * k + 8]))
                    parts = [p * d8 for p, d8 in zip(parts, step8)]
                mix[pl.ds(row, 16), lane] = jnp.concatenate(done, axis=0).astype(BF16)
                return parts

            lax.fori_loop(0, block_rows // 16, rows16, parts)
            return 0

        lax.fori_loop(0, tiles, tile, 0)

    out_cols = w_hbm.shape[1]
    piece_cols = out_cols // (2 * SUB)

    def partial(d, col):
        return jnp.dot(
            mix[pl.ds(pl.multiple_of(d * block_rows, block_rows), block_rows), :],
            w_ref[:, pl.ds(pl.multiple_of(col, piece_cols), piece_cols)],
            preferred_element_type=F32,
        )

    def ring(k, n, sign):
        out, into, ss, rs = (
            (cw_out, cw_in, cw_ss, cw_rs) if sign > 0 else (ccw_out, ccw_in, ccw_ss, ccw_rs)
        )
        return remote(
            out.at[k, n], into.at[k, n], ss.at[k, n], rs.at[k, n], tp=tp_at(sign)
        )

    for k in range(n_tp):
        if k == 0:
            mix_block(tp_at(-1))
            mix_block(tp_at(1))
        elif k == 1:
            mix_block(tp_at(2))
        elif k == 3:
            mix_block(me)

        def pieces(n, _, k=k):
            for sign, out, into in ((1, cw_out, cw_in), (-1, ccw_out, ccw_in)):
                col = n * piece_cols + (0 if sign > 0 else SUB * piece_cols)
                total = partial(tp_at(-sign * (k + 1)), col)
                if k > 0:
                    ring(k - 1, n, sign).wait_recv()
                    total += into[k - 1, n].astype(F32)
                if k < n_tp - 1:
                    out[k, n] = total.astype(BF16)
                    ring(k, n, sign).start()
                else:
                    out_ref[:, pl.ds(pl.multiple_of(col, piece_cols), piece_cols)] = total.astype(
                        BF16
                    )
            return 0

        lax.fori_loop(0, SUB, pieces, 0)

    for copy in tails + halos_g + halos_f + [near] + fars + downs:
        copy.wait_send()
    for k in range(n_tp - 1):

        def drain(n, _, k=k):
            ring(k, n, 1).wait_send()
            ring(k, n, -1).wait_send()
            return 0

        lax.fori_loop(0, SUB, drain, 0)


def shards(
    n_seq, n_tp, tokens, seg_length, seg_offset, short_weight, residues, spans, skip_gain, out_weight
):
    buf_rows, _, chans = tokens.shape
    rows = buf_rows // 2
    half = rows // 2
    modes = residues.shape[0]
    tiles = chans // LANES
    group = min(ROW_GROUP, n_seq)
    cols = n_seq // group
    out_cols = out_weight.shape[1]
    block_rows = rows // n_tp
    vmem = pl.BlockSpec(memory_space=pltpu.VMEM)
    smem = pl.BlockSpec(memory_space=pltpu.SMEM)
    hbm = pl.BlockSpec(memory_space=pl.ANY)
    piece = (n_tp - 1, SUB, block_rows, out_cols // (2 * SUB))
    dma = pltpu.SemaphoreType.DMA
    return pl.pallas_call(
        functools.partial(kernel, n_seq, n_tp),
        out_shape=jax.ShapeDtypeStruct((block_rows, out_cols), BF16),
        in_specs=[smem, smem, hbm, vmem, vmem, vmem, vmem, hbm],
        out_specs=vmem,
        scratch_shapes=[
            pltpu.VMEM((HEAD + buf_rows, chans), BF16),
            pltpu.VMEM((HEAD + buf_rows, chans), BF16),
            pltpu.VMEM((HEAD + buf_rows, chans), BF16),
            pltpu.VMEM((chans, out_cols), BF16),
            pltpu.VMEM((8, chans), F32),
            pltpu.VMEM((2, 8, chans), F32),
            pltpu.VMEM((buf_rows, chans), BF16),
            pltpu.VMEM((buf_rows, chans), BF16),
            pltpu.VMEM((buf_rows, chans), BF16),
            pltpu.VMEM((buf_rows, chans), BF16),
            pltpu.VMEM((half, chans), BF16),
            pltpu.VMEM((half, chans), BF16),
            pltpu.VMEM((half, chans), BF16),
            pltpu.VMEM((half, chans), BF16),
            pltpu.VMEM((modes, chans), F32),
            pltpu.VMEM((modes, chans), F32),
            pltpu.VMEM((modes, chans), F32),
            pltpu.VMEM((modes, chans), F32),
            pltpu.VMEM((group - 1, modes, chans), F32),
            pltpu.VMEM((2, modes, chans), F32),
            pltpu.VMEM((cols - 1, modes, chans), F32),
            pltpu.VMEM((modes, chans), F32),
            pltpu.VMEM((modes * tiles, LANES), F32),
            pltpu.VMEM((modes * tiles, LANES), F32),
            pltpu.VMEM((rows * tiles, LANES), F32),
            pltpu.VMEM((rows * tiles, LANES), F32),
            pltpu.VMEM((rows, chans), BF16),
            pltpu.VMEM(piece, BF16),
            pltpu.VMEM(piece, BF16),
            pltpu.VMEM(piece, BF16),
            pltpu.VMEM(piece, BF16),
            dma((4,)),
            dma((2,)),
            dma((2,)),
            dma((4,)),
            dma((4,)),
            dma,
            dma,
            dma((group - 1,)),
            dma((group - 1,)),
            dma((cols - 1,)),
            dma((cols - 1,)),
            dma(piece[:2]),
            dma(piece[:2]),
            dma(piece[:2]),
            dma(piece[:2]),
        ],
        compiler_params=pltpu.CompilerParams(
            collective_id=0, has_side_effects=True, vmem_limit_bytes=56 * 1024 * 1024
        ),
        name="hyena_mixer",
    )(
        seg_length,
        seg_offset,
        jnp.transpose(tokens, (1, 0, 2)),
        short_weight,
        residues,
        spans,
        skip_gain[None, :],
        out_weight,
    )


def solution(mesh):
    in_specs = (
        P("seq", None, "tp"),
        P("seq"),
        P("seq"),
        P(None, None, "tp"),
        P(None, "tp"),
        P(None, "tp"),
        P("tp"),
        P("tp", None),
    )
    out_specs = P(("seq", "tp"), None)
    body = functools.partial(shards, mesh.shape["seq"], mesh.shape["tp"])
    return jax.shard_map(body, mesh=mesh, in_specs=in_specs, out_specs=out_specs, check_vma=False)
```

```python
import functools

import jax
import jax.numpy as jnp
from jax import lax
from jax.experimental import pallas as pl
from jax.experimental.pallas import tpu as pltpu
from jax.sharding import PartitionSpec as P

F32 = jnp.float32
BF16 = jnp.bfloat16
LANES = 128
ROW_GROUP = 8
HEAD = 8
CHUNK = 64
SUB = 4


def remote(src, dst, send_sem, recv_sem, **where):
    return pltpu.make_async_remote_copy(
        src_ref=src,
        dst_ref=dst,
        send_sem=send_sem,
        recv_sem=recv_sem,
        device_id=where,
        device_id_type=pl.DeviceIdType.MESH,
    )


def add_all(terms):
    while len(terms) > 1:
        terms = [a + b for a, b in zip(terms[::2], terms[1::2])] + (
            [terms[-1]] if len(terms) % 2 else []
        )
    return terms[0]


def kernel(
    n_seq,
    n_tp,
    len_ref,
    off_ref,
    x_hbm,
    taps_ref,
    res_ref,
    span_ref,
    skip_ref,
    w_hbm,
    out_ref,
    xq,
    xk,
    xv,
    w_ref,
    q_t,
    k_t,
    v_t,
    taps_t,
    tail_out,
    tail_in,
    qtail_out,
    qtail_in,
    g_t,
    f_t,
    g_out,
    g_in,
    f_out,
    f_in,
    own_state,
    near_out,
    near_in,
    far_out,
    far_in,
    col_out,
    col_in,
    carry_ref,
    rate_t,
    weight_t,
    skip_t,
    y_t,
    mix,
    cw_out,
    cw_in,
    ccw_out,
    ccw_in,
    load_sem,
    tail_ss,
    tail_rs,
    qtail_ss,
    qtail_rs,
    halo_ss,
    halo_rs,
    near_ss,
    near_rs,
    far_ss,
    far_rs,
    col_ss,
    col_rs,
    cw_ss,
    cw_rs,
    ccw_ss,
    ccw_rs,
):
    buf_rows = x_hbm.shape[1]
    rows = buf_rows // 2
    half = rows // 2
    chans = x_hbm.shape[2]
    modes = res_ref.shape[0]
    tiles = chans // LANES
    group = min(ROW_GROUP, n_seq)
    cols = n_seq // group
    s = lax.axis_index("seq")
    me = lax.axis_index("tp")
    row_id = lax.div(s, group)
    pos = lax.rem(s, group)

    def seq_at(k):
        return lax.rem(s + k + n_seq, n_seq)

    def mate(k):
        return row_id * group + lax.rem(pos + k, group)

    def below(k):
        return lax.rem(row_id + k, cols) * group + pos

    def tp_at(k):
        return lax.rem(me + k + n_tp, n_tp)

    loads = [
        pltpu.make_async_copy(x_hbm.at[j], ref, load_sem.at[j])
        for j, ref in ((1, xk), (2, xv), (0, xq))
    ]
    loads.append(pltpu.make_async_copy(w_hbm, w_ref, load_sem.at[3]))
    for copy in loads:
        copy.start()

    barrier = pltpu.get_barrier_semaphore()
    greeted = 0
    for k in (1, -1, 2, -2):
        pl.semaphore_signal(barrier, inc=1, device_id={"seq": seq_at(k)}, device_id_type=pl.DeviceIdType.MESH)
        greeted += 1
    for k in range(1, group):
        pl.semaphore_signal(barrier, inc=1, device_id={"seq": mate(k)}, device_id_type=pl.DeviceIdType.MESH)
        greeted += 1
    for k in range(1, cols):
        pl.semaphore_signal(barrier, inc=1, device_id={"seq": below(k)}, device_id_type=pl.DeviceIdType.MESH)
        greeted += 1
    for k in (1, -1):
        pl.semaphore_signal(barrier, inc=1, device_id={"tp": tp_at(k)}, device_id_type=pl.DeviceIdType.MESH)
        greeted += 1

    seg_len = jnp.clip(len_ref[0], 0, buf_rows)
    shift = jnp.clip(off_ref[0] - (rows * s - half), 0, rows)

    for j in range(tiles):
        lane = pl.ds(j * LANES, LANES)
        rate = 1.0 / span_ref[:, lane]
        rate_t[:, j, :] = rate
        weight_t[:, j, :] = res_ref[:, lane] * jnp.sqrt(rate)
        skip_t[pl.ds(j, 1), :] = skip_ref[:, lane]
        for i in range(3):
            for n in range(3):
                taps_t[3 * n + i, pl.ds(j, 1), :] = taps_ref[i, pl.ds(n, 1), lane]
    pad = rows + HEAD
    for ref in (k_t, v_t, q_t):
        ref[pl.ds(0, pad)] = jnp.zeros((pad, tiles, LANES), F32)

    def spread(copy, src, dst):
        copy.wait()

        def step(m, _):
            for j in range(tiles):
                dst[pl.ds(pad + CHUNK * m, CHUNK), j, :] = src[
                    pl.ds(pl.multiple_of(CHUNK * m, CHUNK), CHUNK), pl.ds(j * LANES, LANES)
                ].astype(F32)
            return 0

        lax.fori_loop(0, buf_rows // CHUNK, step, 0)

    def send_tails(out, into, ss, rs):
        copies = [
            remote(out, into.at[k - 1], ss.at[k - 1], rs.at[k - 1], seq=seq_at(k)) for k in (1, 2)
        ]
        for copy in copies:
            copy.start()
        return copies

    spread(loads[0], xk, k_t)
    spread(loads[1], xv, v_t)
    tail_out[4] = jnp.full((tiles, LANES), jnp.minimum(seg_len, 2).astype(F32))
    for n, ref in enumerate((k_t, v_t)):
        for k in range(2):
            tail_out[2 * n + k] = ref[pad - 2 + k + seg_len]
    pl.semaphore_wait(barrier, greeted)
    tails = send_tails(tail_out, tail_in, tail_ss, tail_rs)
    spread(loads[2], xq, q_t)
    for k in range(2):
        qtail_out[k] = q_t[pad - 2 + k + seg_len]
    qtails = send_tails(qtail_out, qtail_in, qtail_ss, qtail_rs)

    def put_tail(dst, into, n):
        count = tail_in[0, 4]
        last = jnp.where(count > 0.5, into[0, 2 * n + 1], jnp.where(s > 1, into[1, 2 * n + 1], 0.0))
        prev = jnp.where(
            count > 1.5,
            into[0, 2 * n],
            jnp.where(s > 1, jnp.where(count > 0.5, into[1, 2 * n + 1], into[1, 2 * n]), 0.0),
        )
        dst[pad - 1] = jnp.where(s > 0, last, 0.0)
        dst[pad - 2] = jnp.where(s > 0, prev, 0.0)

    reach = 0.5 * seg_len.astype(F32)
    middle = reach - 0.5 + shift.astype(F32)

    def pairs_of(first, stop, sources, store):
        def load(ref, u):
            return ref[pad - shift + u]

        def step(v, held):
            away, *past = held
            u = 2 * v
            values = []
            later = []
            for (ref, taps), (before, last) in zip(sources, past):
                x = [before, last, load(ref, u), load(ref, u + 1)]
                values.append(
                    [taps[0] * x[k + 2] + taps[1] * x[k + 1] + taps[2] * x[k] for k in range(2)]
                )
                later.append((x[2], x[3]))
            kept = []
            for k in range(2):
                value = values[0][k]
                for other in values[1:]:
                    value = value * other[k]
                kept.append(jnp.where(jnp.abs(away + k) < reach, value, 0.0))
            store(u, kept)
            return (away + 2.0, *later)

        away = jnp.zeros((tiles, LANES), F32) + (first - middle)
        past = [(load(ref, first - 2), load(ref, first - 1)) for ref, _ in sources]
        lax.fori_loop(first // 2, stop // 2, step, (away, *past), unroll=4)

    taps = [[taps_t[3 * n + i] for i in range(3)] for n in range(3)]

    def gate(first, stop, at=None):
        def store(u, kept):
            pair = jnp.concatenate(kept, axis=0).astype(BF16)
            if at is not None:
                place = pl.multiple_of((u - first + at) * tiles, 2 * tiles)
                g_out[pl.ds(place, 2 * tiles), :] = pair
            wide = pair.astype(F32)
            g_t[u] = wide[:tiles]
            g_t[u + 1] = wide[tiles:]

        pairs_of(first, stop, [(k_t, taps[1]), (v_t, taps[2])], store)

    def query(first, stop, at=None):
        def store(u, kept):
            if at is not None:
                place = pl.multiple_of((u - first + at) * tiles, 2 * tiles)
                f_out[pl.ds(place, 2 * tiles), :] = jnp.concatenate(kept, axis=0).astype(BF16)
            else:
                f_t[u - half] = kept[0]
                f_t[u - half + 1] = kept[1]

        pairs_of(first, stop, [(q_t, taps[0])], store)

    def halo(out, into, k):
        size = half * tiles
        low, high = pl.ds(0, size), pl.ds(size, size)
        return [
            remote(out.at[low], into.at[low], halo_ss.at[k], halo_rs.at[k], seq=seq_at(1)),
            remote(
                out.at[high], into.at[high], halo_ss.at[k + 1], halo_rs.at[k + 1], seq=seq_at(-1)
            ),
        ]

    halos_g = halo(g_out, g_in, 0)
    halos_f = halo(f_out, f_in, 2)
    free = rows + 8
    gate(half + rows, buf_rows, 0)
    halos_g[0].start()
    gate(free, half + rows)
    query(half + rows, buf_rows, 0)
    query(free, half + rows)
    for copy in tails:
        copy.wait_recv()
    put_tail(k_t, tail_in, 0)
    put_tail(v_t, tail_in, 1)
    gate(0, half, half)
    halos_g[1].start()
    gate(half, free)

    rate = rate_t[...]
    decay1 = jnp.exp(-rate)
    decays = [decay1[r] for r in range(modes)]

    def accumulate(u, held):
        g = g_t[u]
        return [h * d + g for h, d in zip(held, decays)]

    flat = (modes * tiles, LANES)
    shaped = (modes, tiles, LANES)
    held = [jnp.zeros((tiles, LANES), F32)] * modes
    held = lax.fori_loop(0, half, accumulate, held, unroll=8)
    for r in range(modes):
        own_state[r] = held[r] * decays[r]
    held = lax.fori_loop(half, half + rows, accumulate, held, unroll=8)
    near_out[...] = jnp.concatenate([h * d for h, d in zip(held, decays)], axis=0).astype(BF16)
    held = lax.fori_loop(half + rows, buf_rows, accumulate, held, unroll=8)
    ahead = jnp.exp(float(half - rows - 1) * rate)
    whole = jnp.concatenate([held[r] * ahead[r] for r in range(modes)], axis=0).astype(BF16)
    far_out[...] = whole

    fars = [
        remote(far_out, far_in.at[k - 1], far_ss.at[k - 1], far_rs.at[k - 1], seq=mate(k))
        for k in range(1, group)
    ]
    for copy in fars:
        copy.start()
    near = remote(near_out, near_in, near_ss, near_rs, seq=seq_at(1))
    near.start()

    for copy in qtails:
        copy.wait_recv()
    put_tail(q_t, qtail_in, 0)
    query(0, half, half)
    query(half, free)
    for copy in fars:
        copy.wait_send()
    for copy in halos_f:
        copy.start()

    for copy in halos_g:
        copy.wait_recv()
    weights = [weight_t[r] for r in range(modes)]
    skip = skip_t[...]

    def pair_of(src, into, u):
        other = into[pl.ds(pl.multiple_of(u * tiles, 2 * tiles), 2 * tiles), :].astype(F32)
        return src[u] + other[:tiles], src[u + 1] + other[tiles:]

    def tokens(v, held):
        for k, g in enumerate(pair_of(g_t.at[pl.ds(half, rows)], g_in, 2 * v)):
            held = [h * d + g for h, d in zip(held, decays)]
            y_t[2 * v + k] = add_all([h * w for h, w in zip(held, weights)] + [skip * g])
        return held

    local = [jnp.zeros((tiles, LANES), F32)] * modes
    local = lax.fori_loop(0, rows // 4, tokens, local, unroll=2)

    def powers(blocks):
        return jnp.exp((-float(rows) * blocks.astype(F32)) * rate)

    for copy in fars:
        copy.wait_recv()
    carry = jnp.zeros_like(rate)
    mine = far_out[...].astype(F32).reshape(shaped)
    row_sum = powers(group - 1 - pos) * mine
    row_short = jnp.where(
        pos < group - 1, powers(jnp.maximum(group - 2 - pos, 0)) * mine, 0.0
    )
    for k in range(1, group):
        source = lax.rem(pos - k + group, group)
        piece = far_in[k - 1].astype(F32).reshape(shaped)
        row_sum += powers(group - 1 - source) * piece
        row_short += jnp.where(
            source < group - 1, powers(jnp.maximum(group - 2 - source, 0)) * piece, 0.0
        )
        if k >= 2:
            carry += jnp.where(k <= pos, powers(jnp.int32(k - 2)) * piece, 0.0)
    first_down = jnp.where(pos == 0, row_short, powers(jnp.maximum(pos - 1, 0)) * row_sum)
    col_out[0] = first_down.reshape(flat).astype(BF16)
    col_out[1] = (powers(group + pos - 1) * row_sum).reshape(flat).astype(BF16)
    downs = [
        remote(
            col_out.at[min(k - 1, 1)],
            col_in.at[k - 1],
            col_ss.at[k - 1],
            col_rs.at[k - 1],
            seq=below(k),
        )
        for k in range(1, cols)
    ]
    for copy in downs:
        copy.start()

    lax.fori_loop(rows // 4, rows // 2, tokens, local, unroll=2)

    near.wait_recv()
    carry += own_state[...]
    carry += jnp.where(s > 0, near_in[...].astype(F32).reshape(shaped), 0.0)
    for k, copy in enumerate(downs, 1):
        copy.wait_recv()
        piece = col_in[k - 1].astype(F32).reshape(shaped)
        if k > 2:
            piece = piece * jnp.exp(-float(rows * group * (k - 2)) * rate)
        carry += jnp.where(k <= row_id, piece, 0.0)
    carry_ref[...] = carry * weight_t[...]

    for copy in halos_f:
        copy.wait_recv()
    loads[3].wait()

    block_rows = rows // n_tp

    def mix_block(d):
        first = d * block_rows
        ahead = jnp.exp(-first.astype(F32) * rate_t[...])
        parts = [carry_ref[r] * ahead[r] for r in range(modes)]

        def pairs(v, parts):
            u = first + 2 * v
            for k, f in enumerate(pair_of(f_t, f_in, u)):
                y_t[u + k] = f * add_all(parts + [y_t[u + k]])
                parts = [p * d1 for p, d1 in zip(parts, decays)]
            return parts

        lax.fori_loop(0, block_rows // 2, pairs, parts, unroll=2)

        def lay(m, _):
            row = pl.multiple_of(first + 16 * m, 16)
            for j in range(tiles):
                mix[pl.ds(row, 16), pl.ds(j * LANES, LANES)] = y_t[pl.ds(row, 16), j, :].astype(
                    BF16
                )
            return 0

        lax.fori_loop(0, block_rows // 16, lay, 0, unroll=2)

    out_cols = w_hbm.shape[1]
    piece_cols = out_cols // (2 * SUB)

    def partial(d, col):
        return jnp.dot(
            mix[pl.ds(pl.multiple_of(d * block_rows, block_rows), block_rows), :],
            w_ref[:, pl.ds(pl.multiple_of(col, piece_cols), piece_cols)],
            preferred_element_type=F32,
        )

    def ring(k, n, sign):
        out, into, ss, rs = (
            (cw_out, cw_in, cw_ss, cw_rs) if sign > 0 else (ccw_out, ccw_in, ccw_ss, ccw_rs)
        )
        return remote(
            out.at[k, n], into.at[k, n], ss.at[k, n], rs.at[k, n], tp=tp_at(sign)
        )

    for k in range(n_tp):

        def pieces(n, _, k=k, signs=(1, -1)):
            for sign in signs:
                out, into = (cw_out, cw_in) if sign > 0 else (ccw_out, ccw_in)
                col = n * piece_cols + (0 if sign > 0 else SUB * piece_cols)
                total = partial(tp_at(-sign * (k + 1)), col)
                if k > 0:
                    ring(k - 1, n, sign).wait_recv()
                    total += into[k - 1, n].astype(F32)
                if k < n_tp - 1:
                    out[k, n] = total.astype(BF16)
                    ring(k, n, sign).start()
                else:
                    out_ref[:, pl.ds(pl.multiple_of(col, piece_cols), piece_cols)] = total.astype(
                        BF16
                    )
            return 0

        if k == 0:
            mix_block(tp_at(-1))
            pieces(0, 0, signs=(1,))
            mix_block(tp_at(1))
            pieces(0, 0, signs=(-1,))
            lax.fori_loop(1, SUB, pieces, 0)
            mix_block(tp_at(2))
        else:
            lax.fori_loop(0, SUB, pieces, 0)
            if k == 1:
                mix_block(me)

    for copy in tails + qtails + halos_g + halos_f + [near] + downs:
        copy.wait_send()
    for k in range(n_tp - 1):

        def drain(n, _, k=k):
            ring(k, n, 1).wait_send()
            ring(k, n, -1).wait_send()
            return 0

        lax.fori_loop(0, SUB, drain, 0)


def shards(
    n_seq, n_tp, tokens, seg_length, seg_offset, short_weight, residues, spans, skip_gain, out_weight
):
    buf_rows, _, chans = tokens.shape
    rows = buf_rows // 2
    modes = residues.shape[0]
    tiles = chans // LANES
    group = min(ROW_GROUP, n_seq)
    cols = n_seq // group
    out_cols = out_weight.shape[1]
    block_rows = rows // n_tp
    vmem = pl.BlockSpec(memory_space=pltpu.VMEM)
    smem = pl.BlockSpec(memory_space=pltpu.SMEM)
    hbm = pl.BlockSpec(memory_space=pl.ANY)
    piece = (n_tp - 1, SUB, block_rows, out_cols // (2 * SUB))
    dma = pltpu.SemaphoreType.DMA
    state = (modes, tiles, LANES)
    flat = (modes * tiles, LANES)
    return pl.pallas_call(
        functools.partial(kernel, n_seq, n_tp),
        out_shape=jax.ShapeDtypeStruct((block_rows, out_cols), BF16),
        in_specs=[smem, smem, hbm, vmem, vmem, vmem, vmem, hbm],
        out_specs=vmem,
        scratch_shapes=[
            pltpu.VMEM((buf_rows, chans), BF16),
            pltpu.VMEM((buf_rows, chans), BF16),
            pltpu.VMEM((buf_rows, chans), BF16),
            pltpu.VMEM((chans, out_cols), BF16),
            pltpu.VMEM((rows + HEAD + buf_rows, tiles, LANES), F32),
            pltpu.VMEM((rows + HEAD + buf_rows, tiles, LANES), F32),
            pltpu.VMEM((rows + HEAD + buf_rows, tiles, LANES), F32),
            pltpu.VMEM((9, tiles, LANES), F32),
            pltpu.VMEM((5, tiles, LANES), F32),
            pltpu.VMEM((2, 5, tiles, LANES), F32),
            pltpu.VMEM((2, tiles, LANES), F32),
            pltpu.VMEM((2, 2, tiles, LANES), F32),
            pltpu.VMEM((buf_rows, tiles, LANES), F32),
            pltpu.VMEM((rows, tiles, LANES), F32),
            pltpu.VMEM((rows * tiles, LANES), BF16),
            pltpu.VMEM((rows * tiles, LANES), BF16),
            pltpu.VMEM((rows * tiles, LANES), BF16),
            pltpu.VMEM((rows * tiles, LANES), BF16),
            pltpu.VMEM(state, F32),
            pltpu.VMEM(flat, BF16),
            pltpu.VMEM(flat, BF16),
            pltpu.VMEM(flat, BF16),
            pltpu.VMEM((group - 1, *flat), BF16),
            pltpu.VMEM((2, *flat), BF16),
            pltpu.VMEM((cols - 1, *flat), BF16),
            pltpu.VMEM(state, F32),
            pltpu.VMEM(state, F32),
            pltpu.VMEM(state, F32),
            pltpu.VMEM((tiles, LANES), F32),
            pltpu.VMEM((rows, tiles, LANES), F32),
            pltpu.VMEM((rows, chans), BF16),
            pltpu.VMEM(piece, BF16),
            pltpu.VMEM(piece, BF16),
            pltpu.VMEM(piece, BF16),
            pltpu.VMEM(piece, BF16),
            dma((4,)),
            dma((2,)),
            dma((2,)),
            dma((2,)),
            dma((2,)),
            dma((4,)),
            dma((4,)),
            dma,
            dma,
            dma((group - 1,)),
            dma((group - 1,)),
            dma((cols - 1,)),
            dma((cols - 1,)),
            dma(piece[:2]),
            dma(piece[:2]),
            dma(piece[:2]),
            dma(piece[:2]),
        ],
        compiler_params=pltpu.CompilerParams(
            collective_id=0, has_side_effects=True, vmem_limit_bytes=60 * 1024 * 1024
        ),
        name="hyena_mixer",
    )(
        seg_length,
        seg_offset,
        jnp.transpose(tokens, (1, 0, 2)),
        short_weight,
        residues,
        spans,
        skip_gain[None, :],
        out_weight,
    )


def solution(mesh):
    in_specs = (
        P("seq", None, "tp"),
        P("seq"),
        P("seq"),
        P(None, None, "tp"),
        P(None, "tp"),
        P(None, "tp"),
        P("tp"),
        P("tp", None),
    )
    out_specs = P(("seq", "tp"), None)
    body = functools.partial(shards, mesh.shape["seq"], mesh.shape["tp"])
    return jax.shard_map(body, mesh=mesh, in_specs=in_specs, out_specs=out_specs, check_vma=False)
```

```python
import functools

import jax
import jax.numpy as jnp
from jax import lax
from jax.experimental import pallas as pl
from jax.experimental.pallas import tpu as pltpu
from jax.sharding import PartitionSpec as P

F32 = jnp.float32
BF16 = jnp.bfloat16
LANES = 128
ROW_GROUP = 8
HEAD = 8
FEW = 4
BATCH = 8
CHUNK = 32
SUB = 4
FLIGHT = 2


def remote(src, dst, send_sem, recv_sem, **where):
    return pltpu.make_async_remote_copy(
        src_ref=src,
        dst_ref=dst,
        send_sem=send_sem,
        recv_sem=recv_sem,
        device_id=where,
        device_id_type=pl.DeviceIdType.MESH,
    )


def add_all(terms):
    while len(terms) > 1:
        terms = [a + b for a, b in zip(terms[::2], terms[1::2])] + (
            [terms[-1]] if len(terms) % 2 else []
        )
    return terms[0]


def kernel(
    n_seq,
    n_tp,
    len_ref,
    off_ref,
    x_hbm,
    taps_ref,
    res_ref,
    span_ref,
    skip_ref,
    w_hbm,
    out_ref,
    x_ref,
    w_ref,
    x_t,
    taps_t,
    tail_out,
    tail_in,
    g_win,
    g_in,
    f_win,
    f_in,
    snaps,
    near_out,
    near_in,
    far_out,
    far_in,
    sums,
    col_out,
    col_in,
    carry_ref,
    rate_t,
    weight_t,
    skip_t,
    y_t,
    mix,
    ring_out,
    ring_in,
    load_sem,
    tail_ss,
    tail_rs,
    halo_ss,
    halo_rs,
    near_ss,
    near_rs,
    far_ss,
    far_rs,
    col_ss,
    col_rs,
    ring_ss,
    ring_rs,
):
    buf_rows = x_hbm.shape[1]
    rows = buf_rows // 2
    half = rows // 2
    chans = x_hbm.shape[2]
    modes = res_ref.shape[0]
    tiles = chans // LANES
    group = min(ROW_GROUP, n_seq)
    cols = n_seq // group
    pad = rows + HEAD
    flat = (modes * tiles, LANES)
    shaped = (modes, tiles, LANES)
    s = lax.axis_index("seq")
    me = lax.axis_index("tp")
    row_id = lax.div(s, group)
    pos = lax.rem(s, group)

    def seq_at(k):
        return lax.rem(s + k + n_seq, n_seq)

    def mate(k):
        return row_id * group + lax.rem(pos + k, group)

    def below(k):
        return lax.rem(row_id + k, cols) * group + pos

    def tp_at(k):
        return lax.rem(me + k + n_tp, n_tp)

    loads = [
        pltpu.make_async_copy(x_hbm.at[n], x_ref.at[n], load_sem.at[n]) for n in range(3)
    ]
    loads.append(pltpu.make_async_copy(w_hbm, w_ref, load_sem.at[3]))
    for n in (1, 2, 0):
        loads[n].start()

    barrier = pltpu.get_barrier_semaphore()

    def greet(**where):
        pl.semaphore_signal(barrier, inc=1, device_id=where, device_id_type=pl.DeviceIdType.MESH)

    for k in (1, -1, 2, -2):
        greet(seq=seq_at(k))
    for k in range(1, group):
        greet(seq=mate(k))
    for k in range(1, cols):
        greet(seq=below(k))
    for k in (1, -1):
        greet(tp=tp_at(k))

    seg_len = jnp.clip(len_ref[0], 0, buf_rows)
    shift = jnp.clip(off_ref[0] - (rows * s - half), 0, rows)

    for j in range(tiles):
        lane = pl.ds(j * LANES, LANES)
        rate = 1.0 / span_ref[:, lane]
        rate_t[:, j, :] = rate
        weight_t[:, j, :] = res_ref[:, lane] * jnp.sqrt(rate)
        skip_t[pl.ds(j, 1), :] = skip_ref[:, lane]
        for i in range(3):
            for n in range(3):
                taps_t[3 * n + i, pl.ds(j, 1), :] = taps_ref[i, pl.ds(n, 1), lane]

    def clear(m, _):
        for n in range(3):
            x_t[n, pl.ds(HEAD * m, HEAD)] = jnp.zeros((HEAD, tiles, LANES), F32)
        return 0

    lax.fori_loop(0, pad // HEAD, clear, 0)
    piece_rows, piece_cols = ring_in.shape[3:]

    def clear_ring(m, _):
        for sign in range(2):
            for n in range(SUB):
                ring_in[sign, 0, n, pl.ds(pl.multiple_of(16 * m, 16), 16)] = jnp.zeros(
                    (16, piece_cols), BF16
                )
        return 0

    lax.fori_loop(0, piece_rows // 16, clear_ring, 0)

    def spread(t, _):
        n, m = lax.div(t, buf_rows // CHUNK), lax.rem(t, buf_rows // CHUNK)
        block = x_ref[n, pl.ds(pl.multiple_of(CHUNK * m, CHUNK), CHUNK), :].astype(F32)
        x_t[n, pl.ds(pad + CHUNK * m, CHUNK)] = block.reshape(CHUNK, tiles, LANES)
        return 0

    def send_tails(part, k):
        copies = [
            remote(
                tail_out.at[part],
                tail_in.at[i, part],
                tail_ss.at[k + i],
                tail_rs.at[k + i],
                seq=seq_at(i + 1),
            )
            for i in range(2)
        ]
        for copy in copies:
            copy.start()
        return copies

    starts = (5, 0, 2)
    chunks = buf_rows // CHUNK
    loads[1].wait()
    loads[2].wait()
    lax.fori_loop(chunks, 3 * chunks, spread, 0)
    for n in (1, 2):
        for k in range(2):
            tail_out[starts[n] + k] = x_t[n, pad - 2 + k + seg_len]
    tail_out[4] = jnp.full((tiles, LANES), jnp.minimum(seg_len, 2).astype(F32))
    pl.semaphore_wait(barrier, 4 + group - 1 + cols - 1 + 2)
    tails = send_tails(pl.ds(0, 5), 0)
    loads[0].wait()
    loads[3].start()
    lax.fori_loop(0, chunks, spread, 0)
    for k in range(2):
        tail_out[starts[0] + k] = x_t[0, pad - 2 + k + seg_len]
    qtails = send_tails(pl.ds(5, 2), 2)

    def put_tails(streams):
        count = tail_in[0, 4]
        for n in streams:
            at = starts[n]
            far_last = jnp.where(s > 1, tail_in[1, at + 1], 0.0)
            far_prev = jnp.where(s > 1, tail_in[1, at], 0.0)
            last = jnp.where(count > 0.5, tail_in[0, at + 1], far_last)
            prev = jnp.where(
                count > 1.5, tail_in[0, at], jnp.where(count > 0.5, far_last, far_prev)
            )
            x_t[n, pad - 1] = jnp.where(s > 0, last, 0.0)
            x_t[n, pad - 2] = jnp.where(s > 0, prev, 0.0)

    reach = 0.5 * seg_len.astype(F32)
    middle = reach - 0.5 + shift.astype(F32)

    def featured(streams, first, stop, win):
        taps = [[taps_t[3 * n + i] for i in range(3)] for n in streams]

        def load(n, u):
            return x_t[n, pad - shift + u]

        def step(v, held):
            away, *past = held
            u = BATCH * v
            x = [
                [*before, *(load(n, u + k) for k in range(BATCH))]
                for n, before in zip(streams, past)
            ]
            kept = []
            for k in range(BATCH):
                value = None
                for w, r in zip(taps, x):
                    term = w[0] * r[k + 2] + w[1] * r[k + 1] + w[2] * r[k]
                    value = term if value is None else value * term
                kept.append(jnp.where(jnp.abs(away + float(k)) < reach, value, 0.0))
            place = pl.multiple_of(u * tiles, BATCH * tiles)
            win[pl.ds(place, BATCH * tiles), :] = jnp.concatenate(kept, axis=0).astype(BF16)
            return (away + float(BATCH), *((r[-2], r[-1]) for r in x))

        away = jnp.zeros((tiles, LANES), F32) + (first - middle)
        past = [(load(n, first - 2), load(n, first - 1)) for n in streams]
        lax.fori_loop(lax.div(first, BATCH), lax.div(stop, BATCH), step, (away, *past))

    def halo(out, into, k):
        size = half * tiles
        low, high, last = pl.ds(0, size), pl.ds(size, size), pl.ds(3 * size, size)
        return [
            remote(out.at[last], into.at[low], halo_ss.at[k], halo_rs.at[k], seq=seq_at(1)),
            remote(
                out.at[low], into.at[high], halo_ss.at[k + 1], halo_rs.at[k + 1], seq=seq_at(-1)
            ),
        ]

    halos_g = halo(g_win, g_in, 0)
    halos_f = halo(f_win, f_in, 2)

    free = rows + 8

    def front(phase, _):
        first = jnp.where(phase == 0, free, 0)
        stop = jnp.where(phase == 0, buf_rows, free)

        @pl.when(phase == 1)
        def _():
            for copy in tails:
                copy.wait_recv()
            put_tails((1, 2))

        featured((1, 2), first, stop, g_win)

        @pl.when(phase == 0)
        def _():
            halos_g[0].start()
            featured((0,), free, buf_rows, f_win)

        @pl.when(phase == 1)
        def _():
            halos_g[1].start()

        return 0

    lax.fori_loop(0, 2, front, 0)

    def wide(ref, u, count):
        place = pl.multiple_of(u * tiles, count * tiles)
        flat_rows = ref[pl.ds(place, count * tiles), :].astype(F32)
        return [flat_rows[k * tiles : (k + 1) * tiles] for k in range(count)]

    rate = rate_t[...]
    decay1 = jnp.exp(-rate)
    decays = [decay1[r] for r in range(modes)]

    def part(phase, held):
        def accumulate(v, held):
            for g in wide(g_win, BATCH * v, BATCH):
                held = [h * d + g for h, d in zip(held, decays)]
            return held

        first = jnp.where(phase == 0, 0, jnp.where(phase == 1, half, half + rows))
        stop = jnp.where(phase == 0, half, jnp.where(phase == 1, half + rows, buf_rows))
        held = lax.fori_loop(lax.div(first, BATCH), lax.div(stop, BATCH), accumulate, held)
        for r in range(modes):
            snaps[phase, r] = held[r] * decays[r]
        return held

    lax.fori_loop(0, 3, part, [jnp.zeros((tiles, LANES), F32)] * modes)
    far_out[...] = (snaps[2] * jnp.exp(float(half - rows) * rate)).reshape(flat).astype(BF16)
    far_in[0] = far_out[...]
    near_out[...] = snaps[1].reshape(flat).astype(BF16)

    def far(k):
        return remote(far_out, far_in.at[k], far_ss.at[k - 1], far_rs.at[k - 1], seq=mate(k))

    for k in range(1, group):
        far(k).start()
    near = remote(near_out, near_in, near_ss, near_rs, seq=seq_at(1))
    near.start()
    halos_f[0].start()
    for copy in qtails:
        copy.wait_recv()
    put_tails((0,))
    featured((0,), 0, free, f_win)
    halos_f[1].start()

    for copy in halos_g:
        copy.wait_recv()
    weights = [weight_t[r] for r in range(modes)]
    skip = skip_t[...]

    def joined(win, into, u):
        return [a + b for a, b in zip(wide(win, half + u, FEW), wide(into, u, FEW))]

    def tokens(v, held):
        u = FEW * v
        done = []
        for g in joined(g_win, g_in, u):
            held = [h * d + g for h, d in zip(held, decays)]
            done.append(add_all([h * w for h, w in zip(held, weights)] + [skip * g]))
        for k, value in enumerate(done):
            y_t[u + k] = value
        return held

    def local(first, stop, held):
        return lax.fori_loop(first // FEW, stop // FEW, tokens, held)

    for k in range(1, group):
        far(k).wait_send()

    def powers(blocks):
        return jnp.exp((-float(rows) * blocks.astype(F32)) * rate_t[...])

    def gather(k, _):
        source = lax.rem(pos - k + group, group)

        @pl.when(k > 0)
        def _():
            far(jnp.maximum(k, 1)).wait_recv()

        piece = far_in[k].astype(F32).reshape(shaped)
        short = piece * powers(jnp.maximum(group - 2 - source, 0))
        last = source == group - 1
        sums[0] += jnp.where(last, piece, short * powers(jnp.int32(1)))
        sums[1] += jnp.where(last, 0.0, short)
        sums[2] += jnp.where(
            (k >= 2) & (k <= pos), powers(jnp.maximum(k - 2, 0)) * piece, 0.0
        )
        return 0

    for n in range(3):
        sums[n] = jnp.zeros(shaped, F32)
    lax.fori_loop(0, group, gather, 0)
    first_down = jnp.where(pos == 0, sums[1], powers(jnp.maximum(pos - 1, 0)) * sums[0])
    col_out[0] = first_down.reshape(flat).astype(BF16)
    col_out[1] = (powers(group + pos - 1) * sums[0]).reshape(flat).astype(BF16)
    downs = [
        remote(
            col_out.at[min(k - 1, 1)],
            col_in.at[k - 1],
            col_ss.at[k - 1],
            col_rs.at[k - 1],
            seq=below(k),
        )
        for k in range(1, cols)
    ]
    for copy in downs:
        copy.start()

    local(0, rows, [jnp.zeros((tiles, LANES), F32)] * modes)

    near.wait_recv()
    carry = sums[2] + snaps[0]
    carry += jnp.where(s > 0, near_in[...].astype(F32).reshape(shaped), 0.0)
    for k, copy in enumerate(downs, 1):
        copy.wait_recv()
        piece = col_in[k - 1].astype(F32).reshape(shaped)
        if k > 2:
            piece = piece * jnp.exp(-float(rows * group * (k - 2)) * rate_t[...])
        carry += jnp.where(k <= row_id, piece, 0.0)
    carry_ref[...] = carry * weight_t[...]

    for copy in halos_f:
        copy.wait_recv()
    loads[3].wait()

    block_rows = rows // n_tp

    def mix_block(d):
        first = d * block_rows
        ahead = jnp.exp(-first.astype(F32) * rate_t[...])
        parts = [carry_ref[r] * ahead[r] for r in range(modes)]

        def mixed(v, parts):
            u = first + FEW * v
            now = [y_t[u + k] for k in range(FEW)]
            done = []
            for y, f in zip(now, joined(f_win, f_in, u)):
                done.append(f * add_all(parts + [y]))
                parts = [p * d1 for p, d1 in zip(parts, decays)]
            for k, value in enumerate(done):
                y_t[u + k] = value
            return parts

        lax.fori_loop(0, block_rows // FEW, mixed, parts)

        def lay(m, _):
            row = pl.multiple_of(first + 16 * m, 16)
            for j in range(tiles):
                mix[pl.ds(row, 16), pl.ds(j * LANES, LANES)] = y_t[pl.ds(row, 16), j, :].astype(
                    BF16
                )
            return 0

        lax.fori_loop(0, block_rows // 16, lay, 0)

    def ring(way, k, n):
        return remote(
            ring_out.at[way, k, n],
            ring_in.at[way, k + 1, n],
            ring_ss.at[way, k, n],
            ring_rs.at[way, k, n],
            tp=tp_at(1 - 2 * way),
        )

    def pieces(t, _):
        way = lax.rem(t, 2)
        n = lax.rem(lax.div(t, 2), SUB)
        k = lax.div(t, 2 * SUB)
        block = lax.rem(me - (1 - 2 * way) * (k + 1) + 2 * n_tp, n_tp)

        @pl.when((t == 0) | (t == 1) | (t == 2 * SUB) | (t == 6 * SUB))
        def _():
            mix_block(block)

        col = pl.multiple_of((way * SUB + n) * piece_cols, piece_cols)
        total = jnp.dot(
            mix[pl.ds(pl.multiple_of(block * block_rows, block_rows), block_rows), :],
            w_ref[:, pl.ds(col, piece_cols)],
            preferred_element_type=F32,
        )

        @pl.when(k > 0)
        def _():
            ring(way, jnp.maximum(k - 1, 0), n).wait_recv()

        total = (total + ring_in[way, k, n].astype(F32)).astype(BF16)

        @pl.when(k < n_tp - 1)
        def _():
            safe = jnp.minimum(k, n_tp - 2)
            ring_out[way, safe, n] = total

            @pl.when(k * SUB + n >= FLIGHT)
            def _():
                past = jnp.maximum(k * SUB + n - FLIGHT, 0)
                ring(way, lax.div(past, SUB), lax.rem(past, SUB)).wait_send()

            ring(way, safe, n).start()

        @pl.when(k == n_tp - 1)
        def _():
            out_ref[:, pl.ds(col, piece_cols)] = total

        return 0

    lax.fori_loop(0, 2 * SUB * n_tp, pieces, 0)

    for copy in tails + qtails + halos_g + halos_f + [near] + downs:
        copy.wait_send()

    def drain(t, _):
        ring(lax.rem(t, 2), lax.div(t, 2 * SUB), lax.rem(lax.div(t, 2), SUB)).wait_send()
        return 0

    lax.fori_loop(2 * (SUB * (n_tp - 1) - FLIGHT), 2 * SUB * (n_tp - 1), drain, 0)


def shards(
    n_seq, n_tp, tokens, seg_length, seg_offset, short_weight, residues, spans, skip_gain, out_weight
):
    buf_rows, _, chans = tokens.shape
    rows = buf_rows // 2
    modes = residues.shape[0]
    tiles = chans // LANES
    group = min(ROW_GROUP, n_seq)
    cols = n_seq // group
    out_cols = out_weight.shape[1]
    block_rows = rows // n_tp
    vmem = pl.BlockSpec(memory_space=pltpu.VMEM)
    smem = pl.BlockSpec(memory_space=pltpu.SMEM)
    hbm = pl.BlockSpec(memory_space=pl.ANY)
    piece = (SUB, block_rows, out_cols // (2 * SUB))
    dma = pltpu.SemaphoreType.DMA
    state = (modes, tiles, LANES)
    flat = (modes * tiles, LANES)
    return pl.pallas_call(
        functools.partial(kernel, n_seq, n_tp),
        out_shape=jax.ShapeDtypeStruct((block_rows, out_cols), BF16),
        in_specs=[smem, smem, hbm, vmem, vmem, vmem, vmem, hbm],
        out_specs=vmem,
        scratch_shapes=[
            pltpu.VMEM((3, buf_rows, chans), BF16),
            pltpu.VMEM((chans, out_cols), BF16),
            pltpu.VMEM((3, rows + HEAD + buf_rows, tiles, LANES), F32),
            pltpu.VMEM((9, tiles, LANES), F32),
            pltpu.VMEM((7, tiles, LANES), F32),
            pltpu.VMEM((2, 7, tiles, LANES), F32),
            pltpu.VMEM((buf_rows * tiles, LANES), BF16),
            pltpu.VMEM((rows * tiles, LANES), BF16),
            pltpu.VMEM((buf_rows * tiles, LANES), BF16),
            pltpu.VMEM((rows * tiles, LANES), BF16),
            pltpu.VMEM((3, *state), F32),
            pltpu.VMEM(flat, BF16),
            pltpu.VMEM(flat, BF16),
            pltpu.VMEM(flat, BF16),
            pltpu.VMEM((group, *flat), BF16),
            pltpu.VMEM((3, *state), F32),
            pltpu.VMEM((2, *flat), BF16),
            pltpu.VMEM((cols - 1, *flat), BF16),
            pltpu.VMEM(state, F32),
            pltpu.VMEM(state, F32),
            pltpu.VMEM(state, F32),
            pltpu.VMEM((tiles, LANES), F32),
            pltpu.VMEM((rows, tiles, LANES), F32),
            pltpu.VMEM((rows, chans), BF16),
            pltpu.VMEM((2, n_tp - 1, *piece), BF16),
            pltpu.VMEM((2, n_tp, *piece), BF16),
            dma((4,)),
            dma((4,)),
            dma((4,)),
            dma((4,)),
            dma((4,)),
            dma,
            dma,
            dma((group - 1,)),
            dma((group - 1,)),
            dma((cols - 1,)),
            dma((cols - 1,)),
            dma((2, n_tp - 1, SUB)),
            dma((2, n_tp - 1, SUB)),
        ],
        compiler_params=pltpu.CompilerParams(
            collective_id=0, has_side_effects=True, vmem_limit_bytes=60 * 1024 * 1024
        ),
        name="hyena_mixer",
    )(
        seg_length,
        seg_offset,
        jnp.transpose(tokens, (1, 0, 2)),
        short_weight,
        residues,
        spans,
        skip_gain[None, :],
        out_weight,
    )


def solution(mesh):
    in_specs = (
        P("seq", None, "tp"),
        P("seq"),
        P("seq"),
        P(None, None, "tp"),
        P(None, "tp"),
        P(None, "tp"),
        P("tp"),
        P("tp", None),
    )
    out_specs = P(("seq", "tp"), None)
    body = functools.partial(shards, mesh.shape["seq"], mesh.shape["tp"])
    return jax.shard_map(body, mesh=mesh, in_specs=in_specs, out_specs=out_specs, check_vma=False)
```

```python
import functools

import jax
import jax.numpy as jnp
from jax import lax
from jax.experimental import pallas as pl
from jax.experimental.pallas import tpu as pltpu
from jax.sharding import PartitionSpec as P

F32 = jnp.float32
BF16 = jnp.bfloat16
LANES = 128
ROW_GROUP = 8
HEAD = 8
FEW = 4
BATCH = 8
CHUNK = 32
SUB = 4
FLIGHT = 2


def remote(src, dst, send_sem, recv_sem, **where):
    return pltpu.make_async_remote_copy(
        src_ref=src,
        dst_ref=dst,
        send_sem=send_sem,
        recv_sem=recv_sem,
        device_id=where,
        device_id_type=pl.DeviceIdType.MESH,
    )


def add_all(terms):
    while len(terms) > 1:
        terms = [a + b for a, b in zip(terms[::2], terms[1::2])] + (
            [terms[-1]] if len(terms) % 2 else []
        )
    return terms[0]


def kernel(
    n_seq,
    n_tp,
    len_ref,
    off_ref,
    x_hbm,
    taps_ref,
    res_ref,
    span_ref,
    skip_ref,
    w_hbm,
    out_ref,
    x_ref,
    w_ref,
    x_t,
    taps_t,
    tail_out,
    tail_in,
    g_win,
    g_in,
    f_win,
    f_in,
    snaps,
    near_out,
    near_in,
    far_out,
    far_in,
    sums,
    col_out,
    col_in,
    carry_ref,
    rate_t,
    weight_t,
    skip_t,
    y_t,
    mix,
    ring_out,
    ring_in,
    load_sem,
    tail_ss,
    tail_rs,
    halo_ss,
    halo_rs,
    near_ss,
    near_rs,
    far_ss,
    far_rs,
    col_ss,
    col_rs,
    ring_ss,
    ring_rs,
):
    buf_rows = x_hbm.shape[1]
    rows = buf_rows // 2
    half = rows // 2
    chans = x_hbm.shape[2]
    modes = res_ref.shape[0]
    tiles = chans // LANES
    group = min(ROW_GROUP, n_seq)
    cols = n_seq // group
    pad = rows + HEAD
    flat = (modes * tiles, LANES)
    shaped = (modes, tiles, LANES)
    s = lax.axis_index("seq")
    me = lax.axis_index("tp")
    row_id = lax.div(s, group)
    pos = lax.rem(s, group)

    def seq_at(k):
        return lax.rem(s + k + n_seq, n_seq)

    def mate(k):
        return row_id * group + lax.rem(pos + k, group)

    def below(k):
        return lax.rem(row_id + k, cols) * group + pos

    def tp_at(k):
        return lax.rem(me + k + n_tp, n_tp)

    loads = [
        pltpu.make_async_copy(x_hbm.at[n], x_ref.at[n], load_sem.at[n]) for n in range(3)
    ]
    loads.append(pltpu.make_async_copy(w_hbm, w_ref, load_sem.at[3]))
    for n in (1, 2, 0):
        loads[n].start()

    barrier = pltpu.get_barrier_semaphore()

    def greet(**where):
        pl.semaphore_signal(barrier, inc=1, device_id=where, device_id_type=pl.DeviceIdType.MESH)

    for k in (1, -1, 2, -2):
        greet(seq=seq_at(k))
    for k in range(1, group):
        greet(seq=mate(k))
    for k in range(1, cols):
        greet(seq=below(k))
    for k in (1, -1):
        greet(tp=tp_at(k))

    seg_len = jnp.clip(len_ref[0], 0, buf_rows)
    shift = jnp.clip(off_ref[0] - (rows * s - half), 0, rows)

    rate = 1.0 / span_ref[...]
    rate_t[...] = rate.reshape(shaped)
    weight_t[...] = (res_ref[...] * jnp.sqrt(rate)).reshape(shaped)
    for j in range(tiles):
        lane = pl.ds(j * LANES, LANES)
        skip_t[pl.ds(j, 1), :] = skip_ref[:, lane]
        for i in range(3):
            for n in range(3):
                taps_t[3 * n + i, pl.ds(j, 1), :] = taps_ref[i, pl.ds(n, 1), lane]

    def clear(m, _):
        for n in range(3):
            x_t[n, pl.ds(HEAD * m, HEAD)] = jnp.zeros((HEAD, tiles, LANES), F32)
        return 0

    lax.fori_loop(0, pad // HEAD, clear, 0)
    piece_rows, piece_cols = ring_in.shape[3:]

    def clear_ring(m, _):
        for sign in range(2):
            for n in range(SUB):
                ring_in[sign, 0, n, pl.ds(pl.multiple_of(16 * m, 16), 16)] = jnp.zeros(
                    (16, piece_cols), BF16
                )
        return 0

    lax.fori_loop(0, piece_rows // 16, clear_ring, 0)

    def spread(t, _):
        n, m = lax.div(t, buf_rows // CHUNK), lax.rem(t, buf_rows // CHUNK)
        block = x_ref[n, pl.ds(pl.multiple_of(CHUNK * m, CHUNK), CHUNK), :].astype(F32)
        x_t[n, pl.ds(pad + CHUNK * m, CHUNK)] = block.reshape(CHUNK, tiles, LANES)
        return 0

    def send_tails(part, k):
        copies = [
            remote(
                tail_out.at[part],
                tail_in.at[i, part],
                tail_ss.at[k + i],
                tail_rs.at[k + i],
                seq=seq_at(i + 1),
            )
            for i in range(2)
        ]
        for copy in copies:
            copy.start()
        return copies

    starts = (5, 0, 2)
    chunks = buf_rows // CHUNK
    loads[1].wait()
    loads[2].wait()
    lax.fori_loop(chunks, 3 * chunks, spread, 0)
    for n in (1, 2):
        for k in range(2):
            tail_out[starts[n] + k] = x_t[n, pad - 2 + k + seg_len]
    tail_out[4] = jnp.full((tiles, LANES), jnp.minimum(seg_len, 2).astype(F32))
    pl.semaphore_wait(barrier, 4 + group - 1 + cols - 1 + 2)
    tails = send_tails(pl.ds(0, 5), 0)
    loads[0].wait()
    loads[3].start()
    lax.fori_loop(0, chunks, spread, 0)
    for k in range(2):
        tail_out[starts[0] + k] = x_t[0, pad - 2 + k + seg_len]
    qtails = send_tails(pl.ds(5, 2), 2)

    def put_tails(streams):
        count = tail_in[0, 4]
        for n in streams:
            at = starts[n]
            far_last = jnp.where(s > 1, tail_in[1, at + 1], 0.0)
            far_prev = jnp.where(s > 1, tail_in[1, at], 0.0)
            last = jnp.where(count > 0.5, tail_in[0, at + 1], far_last)
            prev = jnp.where(
                count > 1.5, tail_in[0, at], jnp.where(count > 0.5, far_last, far_prev)
            )
            x_t[n, pad - 1] = jnp.where(s > 0, last, 0.0)
            x_t[n, pad - 2] = jnp.where(s > 0, prev, 0.0)

    reach = 0.5 * seg_len.astype(F32)
    middle = reach - 0.5 + shift.astype(F32)

    def featured(streams, first, stop, win):
        taps = [[taps_t[3 * n + i] for i in range(3)] for n in streams]

        def load(n, u):
            return x_t[n, pad - shift + u]

        def step(v, held):
            away, *past = held
            u = BATCH * v
            x = [
                [*before, *(load(n, u + k) for k in range(BATCH))]
                for n, before in zip(streams, past)
            ]
            kept = []
            for k in range(BATCH):
                value = None
                for w, r in zip(taps, x):
                    term = w[0] * r[k + 2] + w[1] * r[k + 1] + w[2] * r[k]
                    value = term if value is None else value * term
                kept.append(jnp.where(jnp.abs(away + float(k)) < reach, value, 0.0))
            place = pl.multiple_of(u * tiles, BATCH * tiles)
            win[pl.ds(place, BATCH * tiles), :] = jnp.concatenate(kept, axis=0).astype(BF16)
            return (away + float(BATCH), *((r[-2], r[-1]) for r in x))

        away = jnp.zeros((tiles, LANES), F32) + (first - middle)
        past = [(load(n, first - 2), load(n, first - 1)) for n in streams]
        lax.fori_loop(lax.div(first, BATCH), lax.div(stop, BATCH), step, (away, *past))

    def halo(out, into, k):
        size = half * tiles
        low, high, last = pl.ds(0, size), pl.ds(size, size), pl.ds(3 * size, size)
        return [
            remote(out.at[last], into.at[low], halo_ss.at[k], halo_rs.at[k], seq=seq_at(1)),
            remote(
                out.at[low], into.at[high], halo_ss.at[k + 1], halo_rs.at[k + 1], seq=seq_at(-1)
            ),
        ]

    halos_g = halo(g_win, g_in, 0)
    halos_f = halo(f_win, f_in, 2)

    free = rows + 8

    def front(phase, _):
        first = jnp.where(phase == 0, free, 0)
        stop = jnp.where(phase == 0, buf_rows, free)

        @pl.when(phase == 1)
        def _():
            for copy in tails:
                copy.wait_recv()
            put_tails((1, 2))

        featured((1, 2), first, stop, g_win)

        @pl.when(phase == 0)
        def _():
            halos_g[0].start()
            featured((0,), free, buf_rows, f_win)

        @pl.when(phase == 1)
        def _():
            halos_g[1].start()

        return 0

    lax.fori_loop(0, 2, front, 0)

    def wide(ref, u, count):
        place = pl.multiple_of(u * tiles, count * tiles)
        flat_rows = ref[pl.ds(place, count * tiles), :].astype(F32)
        return [flat_rows[k * tiles : (k + 1) * tiles] for k in range(count)]

    rate = rate_t[...]
    decay1 = jnp.exp(-rate)
    decays = [decay1[r] for r in range(modes)]

    def part(phase, held):
        def accumulate(v, held):
            for g in wide(g_win, BATCH * v, BATCH):
                held = [h * d + g for h, d in zip(held, decays)]
            return held

        first = jnp.where(phase == 0, 0, jnp.where(phase == 1, half, half + rows))
        stop = jnp.where(phase == 0, half, jnp.where(phase == 1, half + rows, buf_rows))
        held = lax.fori_loop(lax.div(first, BATCH), lax.div(stop, BATCH), accumulate, held)
        for r in range(modes):
            snaps[phase, r] = held[r] * decays[r]
        return held

    lax.fori_loop(0, 3, part, [jnp.zeros((tiles, LANES), F32)] * modes)
    far_out[...] = (snaps[2] * jnp.exp(float(half - rows) * rate)).reshape(flat).astype(BF16)
    far_in[0] = far_out[...]
    near_out[...] = snaps[1].reshape(flat).astype(BF16)

    def far(k):
        return remote(far_out, far_in.at[k], far_ss.at[k - 1], far_rs.at[k - 1], seq=mate(k))

    for k in range(1, group):
        far(k).start()
    near = remote(near_out, near_in, near_ss, near_rs, seq=seq_at(1))
    near.start()
    halos_f[0].start()
    for copy in qtails:
        copy.wait_recv()
    put_tails((0,))
    featured((0,), 0, free, f_win)
    halos_f[1].start()

    for copy in halos_g:
        copy.wait_recv()
    weights = [weight_t[r] for r in range(modes)]
    skip = skip_t[...]

    def joined(win, into, u):
        return [a + b for a, b in zip(wide(win, half + u, FEW), wide(into, u, FEW))]

    def tokens(v, held):
        u = FEW * v
        done = []
        for g in joined(g_win, g_in, u):
            held = [h * d + g for h, d in zip(held, decays)]
            done.append(add_all([h * w for h, w in zip(held, weights)] + [skip * g]))
        for k, value in enumerate(done):
            y_t[u + k] = value
        return held

    def local(first, stop, held):
        return lax.fori_loop(first // FEW, stop // FEW, tokens, held)

    for k in range(1, group):
        far(k).wait_send()

    def powers(blocks):
        return jnp.exp((-float(rows) * blocks.astype(F32)) * rate_t[...])

    def gather(k, _):
        source = lax.rem(pos - k + group, group)

        @pl.when(k > 0)
        def _():
            far(jnp.maximum(k, 1)).wait_recv()

        piece = far_in[k].astype(F32).reshape(shaped)
        short = piece * powers(jnp.maximum(group - 2 - source, 0))
        last = source == group - 1
        sums[0] += jnp.where(last, piece, short * powers(jnp.int32(1)))
        sums[1] += jnp.where(last, 0.0, short)
        sums[2] += jnp.where(
            (k >= 2) & (k <= pos), powers(jnp.maximum(k - 2, 0)) * piece, 0.0
        )
        return 0

    for n in range(3):
        sums[n] = jnp.zeros(shaped, F32)
    lax.fori_loop(0, group, gather, 0)
    first_down = jnp.where(pos == 0, sums[1], powers(jnp.maximum(pos - 1, 0)) * sums[0])
    col_out[0] = first_down.reshape(flat).astype(BF16)
    col_out[1] = (powers(group + pos - 1) * sums[0]).reshape(flat).astype(BF16)
    downs = [
        remote(
            col_out.at[min(k - 1, 1)],
            col_in.at[k - 1],
            col_ss.at[k - 1],
            col_rs.at[k - 1],
            seq=below(k),
        )
        for k in range(1, cols)
    ]
    for copy in downs:
        copy.start()

    local(0, rows, [jnp.zeros((tiles, LANES), F32)] * modes)

    near.wait_recv()
    carry = sums[2] + snaps[0]
    carry += jnp.where(s > 0, near_in[...].astype(F32).reshape(shaped), 0.0)
    for k, copy in enumerate(downs, 1):
        copy.wait_recv()
        piece = col_in[k - 1].astype(F32).reshape(shaped)
        if k > 2:
            piece = piece * jnp.exp(-float(rows * group * (k - 2)) * rate_t[...])
        carry += jnp.where(k <= row_id, piece, 0.0)
    carry_ref[...] = carry * weight_t[...]

    for copy in halos_f:
        copy.wait_recv()
    loads[3].wait()

    block_rows = rows // n_tp

    def mix_block(d):
        first = d * block_rows
        ahead = jnp.exp(-first.astype(F32) * rate_t[...])
        parts = [carry_ref[r] * ahead[r] for r in range(modes)]

        def mixed(v, parts):
            u = first + FEW * v
            now = [y_t[u + k] for k in range(FEW)]
            done = []
            for y, f in zip(now, joined(f_win, f_in, u)):
                done.append(f * add_all(parts + [y]))
                parts = [p * d1 for p, d1 in zip(parts, decays)]
            for k, value in enumerate(done):
                y_t[u + k] = value
            return parts

        lax.fori_loop(0, block_rows // FEW, mixed, parts)

        def lay(m, _):
            row = pl.multiple_of(first + 16 * m, 16)
            mix[pl.ds(row, 16), :] = y_t[pl.ds(row, 16)].reshape(16, chans).astype(BF16)
            return 0

        lax.fori_loop(0, block_rows // 16, lay, 0)

    def ring(way, k, n):
        return remote(
            ring_out.at[way, k, n],
            ring_in.at[way, k + 1, n],
            ring_ss.at[way, k, n],
            ring_rs.at[way, k, n],
            tp=tp_at(1 - 2 * way),
        )

    def pieces(t, _):
        way = lax.rem(t, 2)
        n = lax.rem(lax.div(t, 2), SUB)
        k = lax.div(t, 2 * SUB)
        block = lax.rem(me - (1 - 2 * way) * (k + 1) + 2 * n_tp, n_tp)

        @pl.when((t == 0) | (t == 1) | (t == 2 * SUB) | (t == 6 * SUB))
        def _():
            mix_block(block)

        col = pl.multiple_of((way * SUB + n) * piece_cols, piece_cols)
        total = jnp.dot(
            mix[pl.ds(pl.multiple_of(block * block_rows, block_rows), block_rows), :],
            w_ref[:, pl.ds(col, piece_cols)],
            preferred_element_type=F32,
        )

        @pl.when(k > 0)
        def _():
            ring(way, jnp.maximum(k - 1, 0), n).wait_recv()

        total = (total + ring_in[way, k, n].astype(F32)).astype(BF16)

        @pl.when(k < n_tp - 1)
        def _():
            safe = jnp.minimum(k, n_tp - 2)
            ring_out[way, safe, n] = total

            @pl.when(k * SUB + n >= FLIGHT)
            def _():
                past = jnp.maximum(k * SUB + n - FLIGHT, 0)
                ring(way, lax.div(past, SUB), lax.rem(past, SUB)).wait_send()

            ring(way, safe, n).start()

        @pl.when(k == n_tp - 1)
        def _():
            out_ref[:, pl.ds(col, piece_cols)] = total

        return 0

    lax.fori_loop(0, 2 * SUB * n_tp, pieces, 0)

    for copy in tails + qtails + halos_g + halos_f + [near] + downs:
        copy.wait_send()

    def drain(t, _):
        ring(lax.rem(t, 2), lax.div(t, 2 * SUB), lax.rem(lax.div(t, 2), SUB)).wait_send()
        return 0

    lax.fori_loop(2 * (SUB * (n_tp - 1) - FLIGHT), 2 * SUB * (n_tp - 1), drain, 0)


def shards(
    n_seq, n_tp, tokens, seg_length, seg_offset, short_weight, residues, spans, skip_gain, out_weight
):
    buf_rows, _, chans = tokens.shape
    rows = buf_rows // 2
    modes = residues.shape[0]
    tiles = chans // LANES
    group = min(ROW_GROUP, n_seq)
    cols = n_seq // group
    out_cols = out_weight.shape[1]
    block_rows = rows // n_tp
    vmem = pl.BlockSpec(memory_space=pltpu.VMEM)
    smem = pl.BlockSpec(memory_space=pltpu.SMEM)
    hbm = pl.BlockSpec(memory_space=pl.ANY)
    piece = (SUB, block_rows, out_cols // (2 * SUB))
    dma = pltpu.SemaphoreType.DMA
    state = (modes, tiles, LANES)
    flat = (modes * tiles, LANES)
    return pl.pallas_call(
        functools.partial(kernel, n_seq, n_tp),
        out_shape=jax.ShapeDtypeStruct((block_rows, out_cols), BF16),
        in_specs=[smem, smem, hbm, vmem, vmem, vmem, vmem, hbm],
        out_specs=vmem,
        scratch_shapes=[
            pltpu.VMEM((3, buf_rows, chans), BF16),
            pltpu.VMEM((chans, out_cols), BF16),
            pltpu.VMEM((3, rows + HEAD + buf_rows, tiles, LANES), F32),
            pltpu.VMEM((9, tiles, LANES), F32),
            pltpu.VMEM((7, tiles, LANES), F32),
            pltpu.VMEM((2, 7, tiles, LANES), F32),
            pltpu.VMEM((buf_rows * tiles, LANES), BF16),
            pltpu.VMEM((rows * tiles, LANES), BF16),
            pltpu.VMEM((buf_rows * tiles, LANES), BF16),
            pltpu.VMEM((rows * tiles, LANES), BF16),
            pltpu.VMEM((3, *state), F32),
            pltpu.VMEM(flat, BF16),
            pltpu.VMEM(flat, BF16),
            pltpu.VMEM(flat, BF16),
            pltpu.VMEM((group, *flat), BF16),
            pltpu.VMEM((3, *state), F32),
            pltpu.VMEM((2, *flat), BF16),
            pltpu.VMEM((cols - 1, *flat), BF16),
            pltpu.VMEM(state, F32),
            pltpu.VMEM(state, F32),
            pltpu.VMEM(state, F32),
            pltpu.VMEM((tiles, LANES), F32),
            pltpu.VMEM((rows, tiles, LANES), F32),
            pltpu.VMEM((rows, chans), BF16),
            pltpu.VMEM((2, n_tp - 1, *piece), BF16),
            pltpu.VMEM((2, n_tp, *piece), BF16),
            dma((4,)),
            dma((4,)),
            dma((4,)),
            dma((4,)),
            dma((4,)),
            dma,
            dma,
            dma((group - 1,)),
            dma((group - 1,)),
            dma((cols - 1,)),
            dma((cols - 1,)),
            dma((2, n_tp - 1, SUB)),
            dma((2, n_tp - 1, SUB)),
        ],
        compiler_params=pltpu.CompilerParams(
            collective_id=0, has_side_effects=True, vmem_limit_bytes=60 * 1024 * 1024
        ),
        name="hyena_mixer",
    )(
        seg_length,
        seg_offset,
        jnp.transpose(tokens, (1, 0, 2)),
        short_weight,
        residues,
        spans,
        skip_gain[None, :],
        out_weight,
    )


def solution(mesh):
    in_specs = (
        P("seq", None, "tp"),
        P("seq"),
        P("seq"),
        P(None, None, "tp"),
        P(None, "tp"),
        P(None, "tp"),
        P("tp"),
        P("tp", None),
    )
    out_specs = P(("seq", "tp"), None)
    body = functools.partial(shards, mesh.shape["seq"], mesh.shape["tp"])
    return jax.shard_map(body, mesh=mesh, in_specs=in_specs, out_specs=out_specs, check_vma=False)
```
